32 devices in a mesh: ctx: 8 (over y, x, core), tp: 4 (over z).
Axes of the slice: x: 2, y: 2, z: 4, core: 2. Of those that a mesh axis runs over, the one named last changes fastest.
Arguments:
- queries: bfloat16 [8192, 8192], P(('ctx', 'tp')), may hold values from -36 to 36
- key_rows: bfloat16 [8192, 1024], P(('ctx', 'tp')), may hold values from -6 to 6
- value_rows: bfloat16 [8192, 1024], P(('ctx', 'tp')), may hold values from -6 to 6
- vertical_keys: int32 [8, 1024], P('tp'), may hold values from 0 to 8191, as said below
- slash_offsets: int32 [8, 3], P('tp'), may hold values from 0 to 8128, as said below
Outputs:
- attended: bfloat16 [8192, 8192], P('ctx', 'tp')
The draws below stay inside these ranges and needn't reach their ends.
Inputs may be any that keep to these rules, and one draw needn't show every extreme that they name: `vertical_keys`: each row holds 1024 distinct positions in ascending order; no more than 384 of a row lie in one aligned range of 1024 positions, and in every row some such range holds exactly 384. `slash_offsets`: each row holds 3 distinct multiples of 64, the first of them 0.
All inputs are finite; a program needn't handle non-finite values.
Results may differ from the reference program's by a relative error of at most 0.0035.
Values may be sent and summed in bfloat16 or wider, within the bound.
A program may use at most 320 MiB of HBM per device.

```python
import jax
import jax.numpy as jnp
from jax import lax

HQ = 64
KVH = 8
DH = 128
TOK_DEV = 1024
NVERT = 1024
NBAND = 3
TOKENS = 8192
CAP = 384


def draw_queries(key, part):
    key = jax.random.fold_in(key, 1)
    group_size = HQ // KVH
    base_field = 2.0 * jnp.clip(jax.random.normal(key, (TOKENS, KVH, group_size, DH), jnp.float32), -6.0, 6.0)
    return base_field.reshape(TOKENS, HQ * DH).astype(jnp.bfloat16)


def draw_key_rows(key, part):
    key = jax.random.fold_in(key, 2)
    base_field = jnp.clip(jax.random.normal(key, (TOKENS, KVH, DH), jnp.float32), -6.0, 6.0)
    return base_field.reshape(TOKENS, KVH * DH).astype(jnp.bfloat16)


def draw_vertical_keys(key, part):
    key = jax.random.fold_in(key, 21)
    shards = TOKENS // TOK_DEV
    remaining = NVERT - CAP
    spread = remaining // (shards - 1)
    leftover = remaining % (shards - 1)

    def one_head(head_key):
        first_key, second_key, third_key = jax.random.split(head_key, 3)
        heavy = jax.random.randint(first_key, (), 0, shards)
        jitter = jax.random.randint(second_key, (shards - 1,), 0, spread // 2 + 1)
        order = jnp.arange(shards - 1)
        others = spread + (order < leftover).astype(jnp.int32) + jitter - jnp.roll(jitter, -1)
        slots = jnp.arange(shards)
        lowered = jnp.clip(slots - (slots > heavy).astype(jnp.int32), 0, shards - 2)
        counts = jnp.where(slots == heavy, CAP, others[lowered])
        ranks = jax.vmap(lambda shard_key: jax.random.permutation(shard_key, TOK_DEV))(jax.random.split(third_key, shards))
        chosen = (ranks < counts[:, None]).reshape(TOKENS)
        return jnp.nonzero(chosen, size=NVERT)[0].astype(jnp.int32)
    return jax.vmap(one_head)(jax.random.split(key, KVH))


def draw_slash_offsets(key, part):
    key = jax.random.fold_in(key, 31)
    spots = TOKENS // 64
    first_key, second_key = jax.random.split(key)

    def one_head(head_key):
        return jax.random.permutation(head_key, spots - 2)[:NBAND - 1] + 1
    picks = jax.vmap(one_head)(jax.random.split(first_key, KVH))
    far_head = jax.random.randint(second_key, (), 0, KVH)
    first_col = jnp.where(jnp.arange(KVH) == far_head, spots - 1, picks[:, 0])
    picks = picks.at[:, 0].set(first_col)
    offsets = jnp.concatenate((jnp.zeros((KVH, 1), jnp.int32), picks.astype(jnp.int32)), axis=1)
    return (64 * offsets).astype(jnp.int32)


def block_levels(own_key, shape, cuts, low, high):
    loudness, own = 1.0, jax.random.fold_in(own_key, 6)
    for position, parts in cuts:
        heights = jnp.exp(jax.random.uniform(jax.random.fold_in(own, position), (parts,), jnp.float32, low / len(cuts), high / len(cuts)))
        loudness = loudness * jnp.repeat(heights, shape[position] // parts).reshape([-1 if axis == position else 1 for axis in range(len(shape))])
    return loudness


def bell_draw(stream_key, dims, deviation, most, cuts=(), held_as=jnp.bfloat16):
    loudness = block_levels(stream_key, dims, cuts, -0.22, 0.18) if cuts else 1.0
    array = jax.random.normal(stream_key, dims, jnp.float32) * deviation * loudness
    return jnp.minimum(jnp.maximum(array, -most), most).astype(held_as)


def setup_inputs(seed: int = 0) -> dict:
    keys = jax.random.split(jax.random.key(seed), 6)
    return {
        "queries": draw_queries(jax.random.fold_in(keys[5], 71), 0),
        "key_rows": draw_key_rows(jax.random.fold_in(keys[5], 71), 0),
        "value_rows": bell_draw(keys[2], (TOKENS, KVH * DH), 1.0, 6.0, ((0, 32),)),
        "vertical_keys": draw_vertical_keys(jax.random.fold_in(keys[5], 71), 0),
        "slash_offsets": draw_slash_offsets(jax.random.fold_in(keys[5], 71), 0),
    }


def reference(queries, key_rows, value_rows, vertical_keys, slash_offsets):
    group_size = HQ // KVH
    scale_factor = DH ** -0.5
    key_heads = key_rows.reshape(TOKENS, KVH, DH).transpose(1, 0, 2)
    value_heads = value_rows.reshape(TOKENS, KVH, DH).transpose(1, 0, 2)
    head_ids = jnp.arange(KVH, dtype=jnp.int32)[:, None]
    vert_k = key_heads[head_ids, vertical_keys].astype(jnp.float32)
    vert_v = value_heads[head_ids, vertical_keys].astype(jnp.float32)
    marked = jnp.zeros((KVH, TOKENS), jnp.int32).at[head_ids, vertical_keys].set(1)
    marked_pad = jnp.concatenate((jnp.zeros_like(marked), marked), axis=1)
    pad_zero = jnp.zeros((KVH, TOKENS, DH), jnp.bfloat16)
    key_pad = jnp.concatenate((pad_zero, key_heads), axis=1)
    value_pad = jnp.concatenate((pad_zero, value_heads), axis=1)
    distance = jnp.arange(192, dtype=jnp.int32)[None, :] - jnp.arange(128, dtype=jnp.int32)[:, None]
    in_band = (distance >= 1) & (distance <= 64)

    def cut_tiles(table, firsts):
        return jax.vmap(lambda begin: lax.dynamic_slice_in_dim(table, begin + TOKENS, 192, 0))(firsts)

    def one_block(block_id):
        first_row = block_id * 128
        query_block = lax.dynamic_slice_in_dim(queries, first_row, 128, 0)
        query_block = query_block.reshape(128, KVH, group_size, DH).astype(jnp.float32)
        positions = first_row + jnp.arange(128, dtype=jnp.int32)
        vert_scores = jnp.einsum("qhgd,hnd->hgqn", query_block, vert_k) * scale_factor
        vert_mask = vertical_keys[:, None, None, :] <= positions[None, None, :, None]
        vert_scores = jnp.where(vert_mask, vert_scores, -jnp.inf)
        tile_first = (first_row - slash_offsets - 64).astype(jnp.int32)
        band_k = jax.vmap(cut_tiles)(key_pad, tile_first).astype(jnp.float32)
        band_v = jax.vmap(cut_tiles)(value_pad, tile_first).astype(jnp.float32)
        band_marks = jax.vmap(cut_tiles)(marked_pad, tile_first)
        band_pos = tile_first[:, :, None] + jnp.arange(192, dtype=jnp.int32)[None, None, :]
        band_ok = (band_pos >= 0) & (band_marks == 0)
        band_scores = jnp.einsum("qhgd,hktd->hgqkt", query_block, band_k) * scale_factor
        band_mask = in_band[None, None, :, None, :] & band_ok[:, None, None, :, :]
        band_scores = jnp.where(band_mask, band_scores, -jnp.inf)
        top = jnp.maximum(jnp.max(vert_scores, axis=-1), jnp.max(band_scores, axis=(-2, -1)))
        vert_weight = jnp.exp(vert_scores - top[..., None])
        band_weight = jnp.exp(band_scores - top[..., None, None])
        total = jnp.sum(vert_weight, axis=-1) + jnp.sum(band_weight, axis=(-2, -1))
        vert_round = lax.optimization_barrier(vert_weight.astype(jnp.bfloat16)).astype(jnp.float32)
        band_round = lax.optimization_barrier(band_weight.astype(jnp.bfloat16)).astype(jnp.float32)
        numer = jnp.einsum("hgqn,hnd->hgqd", vert_round, vert_v)
        numer = numer + jnp.einsum("hgqkt,hktd->hgqd", band_round, band_v)
        result = numer / total[..., None]
        return result.transpose(2, 0, 1, 3).reshape(128, HQ * DH).astype(jnp.bfloat16)

    blocks = lax.map(one_block, jnp.arange(TOKENS // 128, dtype=jnp.int32))
    return blocks.reshape(TOKENS, HQ * DH)
```

```python
import functools
import math

import jax
import jax.numpy as jnp
from jax import lax
from jax.experimental import pallas as pl
from jax.experimental.pallas import tpu as pltpu
from jax.sharding import PartitionSpec as P

HQ = 64
KVH = 8
DH = 128
SUB = 64
CHUNKS = 4
VT = 128
PB = 512
EXP2_SCALE = DH**-0.5 * math.log2(math.e)
MASKED = -1e30
VMEM_BYTES = 56 * 1024 * 1024


def gather_body(tok, me_ref, keys_ref, column_ref, kv_ref, vk_ref, vv_ref, marks_ref):
    me = me_ref[0]
    marks_ref[...] = jnp.zeros_like(marks_ref)
    lanes = lax.broadcasted_iota(jnp.int32, (VT, PB), 1)
    for tile in range(keys_ref.shape[0] // VT):
        first = keys_ref[tile * VT] // PB
        last = keys_ref[tile * VT + VT - 1] // PB
        column = column_ref[tile * VT : (tile + 1) * VT, :]

        def add_block(block, total):
            base = block * PB
            place = (lax.bitwise_xor(base // tok, me)) * tok + base % tok
            rows = kv_ref[pl.ds(pl.multiple_of(place, PB), PB), :]
            hit = jnp.where(column - base == lanes, 1.0, 0.0)
            marks_ref[pl.ds(block, 1), :] += jnp.sum(hit, axis=0, keepdims=True)
            return total + jnp.dot(
                hit.astype(jnp.bfloat16), rows, preferred_element_type=jnp.float32
            )

        total = lax.fori_loop(first, last + 1, add_block, jnp.zeros((VT, 2 * DH), jnp.float32))
        total = total.astype(jnp.bfloat16)
        vk_ref[tile * VT : (tile + 1) * VT, :] = total[:, :DH]
        vv_ref[tile * VT : (tile + 1) * VT, :DH] = total[:, DH:]
        vv_ref[tile * VT : (tile + 1) * VT, DH:] = jnp.ones((VT, DH), jnp.bfloat16)


def gather_vertical(me, keys, kv, tok):
    vert = keys.shape[0]
    total = kv.shape[0]
    return pl.pallas_call(
        functools.partial(gather_body, tok),
        out_shape=(
            jax.ShapeDtypeStruct((vert, DH), jnp.bfloat16),
            jax.ShapeDtypeStruct((vert, 2 * DH), jnp.bfloat16),
            jax.ShapeDtypeStruct((total // PB, PB), jnp.float32),
        ),
        in_specs=[
            pl.BlockSpec(memory_space=pltpu.SMEM),
            pl.BlockSpec(memory_space=pltpu.SMEM),
            pl.BlockSpec(memory_space=pltpu.VMEM),
            pl.BlockSpec(memory_space=pltpu.VMEM),
        ],
        out_specs=[pl.BlockSpec(memory_space=pltpu.VMEM)] * 3,
        compiler_params=pltpu.CompilerParams(vmem_limit_bytes=VMEM_BYTES),
        cost_estimate=pl.CostEstimate(flops=8 << 30, bytes_accessed=8 << 20, transcendentals=0),
        name="gather_vertical",
    )(me, keys, keys[:, None], kv)


def attend_body(tok, bands, group, meta_ref, q_ref, row_ref, vk_ref, vv_ref, kv_ref, marks_ref, *rest):
    o_ref = rest[-1]
    me = meta_ref[0]
    per_dev = tok // SUB
    rows = group * SUB
    slots = 4 * SUB
    row_in = lax.broadcasted_iota(jnp.int32, (rows, slots), 0) % SUB
    lane_in = lax.broadcasted_iota(jnp.int32, (rows, slots), 1) % SUB
    upper = lane_in > row_in
    ones = jnp.ones((slots, DH), jnp.bfloat16)
    nt = (((1,), (1,)), ((), ()))
    subs = q_ref.shape[0] // SUB
    for sub in range(subs):
        own = me * per_dev + pl.program_id(0) * subs + sub
        sides = []
        for back in (1, 0):
            blocks, biases = [], []
            for band in range(bands):
                block = own - meta_ref[1 + band] - back
                there = jnp.maximum(block, 0)
                place = lax.bitwise_xor(there // per_dev, me) * per_dev + there % per_dev
                blocks.append(kv_ref[pl.ds(pl.multiple_of(place * SUB, SUB), SUB), :])
                if band == 0 and back == 0:
                    biases.append(jnp.zeros((1, SUB), jnp.float32))
                else:
                    gone = (marks_ref[pl.ds(there, 1), :] > 0.5) | (block < 0)
                    biases.append(jnp.where(gone, MASKED, 0.0))
            for _ in range(4 - bands):
                blocks.append(jnp.zeros((SUB, 2 * DH), jnp.bfloat16))
                biases.append(jnp.full((1, SUB), MASKED, jnp.float32))
            sides.append((jnp.concatenate(blocks, axis=0), jnp.concatenate(biases, axis=1)))
        (near, near_bias), (own_side, own_bias) = sides
        q = jnp.concatenate(
            [q_ref[sub * SUB : (sub + 1) * SUB, g * DH : (g + 1) * DH] for g in range(group)], axis=0
        )
        vert_bias = jnp.where(row_ref[...] < own * SUB, 0.0, MASKED)
        vert = (
            lax.dot_general(q, vk_ref[...], nt, preferred_element_type=jnp.float32) + vert_bias
        )
        s_near = lax.dot_general(q, near[:, :DH], nt, preferred_element_type=jnp.float32)
        s_own = lax.dot_general(q, own_side[:, :DH], nt, preferred_element_type=jnp.float32)
        band = jnp.where(upper, s_near + near_bias, s_own + own_bias)
        top = jnp.maximum(
            jnp.max(vert, axis=1, keepdims=True), jnp.max(band, axis=1, keepdims=True)
        )
        p_vert = jnp.exp2((vert - top) * EXP2_SCALE).astype(jnp.bfloat16)
        p_band = jnp.exp2((band - top) * EXP2_SCALE)
        p_near = jnp.where(upper, p_band, 0.0).astype(jnp.bfloat16)
        p_own = jnp.where(upper, 0.0, p_band).astype(jnp.bfloat16)
        acc = jnp.dot(p_vert, vv_ref[...], preferred_element_type=jnp.float32)
        acc += jnp.dot(
            p_near,
            jnp.concatenate((near[:, DH:], ones), axis=1),
            preferred_element_type=jnp.float32,
        )
        acc += jnp.dot(
            p_own,
            jnp.concatenate((own_side[:, DH:], ones), axis=1),
            preferred_element_type=jnp.float32,
        )
        out = (acc[:, :DH] / acc[:, DH:]).astype(o_ref.dtype)
        for g in range(group):
            o_ref[sub * SUB : (sub + 1) * SUB, g * DH : (g + 1) * DH] = out[
                g * SUB : (g + 1) * SUB
            ]


def attend(meta, q, row, vk, vv, kv, marks, previous, chunk, bands, width):
    tok, columns = q.shape
    group = columns // DH
    block = 128

    def whole(x):
        return pl.BlockSpec(x.shape, lambda i, meta_ref: (0, 0))

    operands = [meta, q, row, vk, vv, kv, marks]
    in_specs = [pl.BlockSpec((block, columns), lambda i, meta_ref: (i, 0))]
    in_specs += [whole(x) for x in operands[2:]]
    aliases = {}
    if previous is not None:
        aliases = {len(operands): 0}
        operands.append(previous)
        in_specs.append(pl.BlockSpec(memory_space=pl.ANY))
    scores = tok * group * 1536
    return pl.pallas_call(
        functools.partial(attend_body, tok, bands, group),
        out_shape=jax.ShapeDtypeStruct((tok, width), jnp.bfloat16),
        grid_spec=pltpu.PrefetchScalarGridSpec(
            num_scalar_prefetch=1,
            grid=(tok // block,),
            in_specs=in_specs,
            out_specs=pl.BlockSpec((block, columns), lambda i, meta_ref: (i, chunk)),
        ),
        input_output_aliases=aliases,
        compiler_params=pltpu.CompilerParams(vmem_limit_bytes=VMEM_BYTES),
        cost_estimate=pl.CostEstimate(
            flops=scores * 1536, bytes_accessed=8 << 20, transcendentals=scores
        ),
        name=f"attend_{chunk}",
    )(*operands)


def gather_ctx(block, order):
    count = lax.axis_size("ctx")
    held = block[None]
    for bit in order:
        route = [(i, i ^ (1 << bit)) for i in range(count)]
        held = jnp.concatenate((held, lax.ppermute(held, "ctx", route)), axis=0)
    bits = len(order)
    held = held.reshape((2,) * bits + block.shape)
    steps = list(reversed(order))
    axes = [steps.index(bit) for bit in reversed(range(bits))]
    held = held.transpose(axes + [bits, bits + 1])
    return held.reshape(count * block.shape[0], block.shape[1])


def shards(queries, key_rows, value_rows, vertical_keys, slash_offsets):
    heads, vert_count = vertical_keys.shape
    bands = slash_offsets.shape[1]
    part = queries.shape[0]
    tp = lax.axis_size("tp")
    count = lax.axis_size("ctx")
    tok = part * tp
    me = lax.axis_index("ctx").astype(jnp.int32)
    width = queries.shape[1] // tp
    step = width // CHUNKS

    kv = jnp.stack(
        (key_rows.reshape(part, tp, heads, DH), value_rows.reshape(part, tp, heads, DH)), axis=3
    )
    kv = kv.transpose(1, 2, 0, 3, 4).reshape(tp, heads, part, 2 * DH)
    kv = lax.all_to_all(kv, "tp", split_axis=0, concat_axis=0)
    q_parts = queries.reshape(part, tp, CHUNKS, step).transpose(2, 1, 0, 3)
    q_send = [q_parts[c] for c in range(CHUNKS)]
    kv, q_send = lax.optimization_barrier((kv, q_send))
    q_got = []
    for c in range(CHUNKS):
        got = lax.all_to_all(q_send[c], "tp", split_axis=0, concat_axis=0)
        if c + 1 < CHUNKS:
            got, q_send[c + 1] = lax.optimization_barrier((got, q_send[c + 1]))
        q_got.append(got.reshape(tok, step))

    bits = max((count - 1).bit_length(), 1)
    orders = (
        list(range(bits - 1, 0, -1)) + [0],
        list(range(1, bits)) + [0],
    )
    tables = []
    for head in range(heads):
        full = gather_ctx(kv[:, head].reshape(tok, 2 * DH), orders[head % 2])
        vk, vv, marks = gather_vertical(me[None], vertical_keys[head], full, tok)
        tables.append((vk, vv, full, marks.reshape(tok * count // SUB, SUB)))

    attended = None
    for c in range(CHUNKS):
        head = c * heads // CHUNKS
        meta = jnp.concatenate((me[None], slash_offsets[head] // SUB))
        attended = attend(
            meta, q_got[c], vertical_keys[head][None], *tables[head], attended, c, bands, width
        )
    return attended


def solution(mesh):
    in_specs = (
        P(("ctx", "tp"), None),
        P(("ctx", "tp"), None),
        P(("ctx", "tp"), None),
        P("tp", None),
        P("tp", None),
    )
    out_specs = P("ctx", "tp")
    return jax.shard_map(shards, mesh=mesh, in_specs=in_specs, out_specs=out_specs, check_vma=False)
```

```python
import functools
import math

import jax
import jax.numpy as jnp
from jax import lax
from jax.experimental import pallas as pl
from jax.experimental.pallas import tpu as pltpu
from jax.sharding import PartitionSpec as P

HQ = 64
KVH = 8
DH = 128
SUB = 64
CHUNKS = 4
VT = 256
PB = 512
EXP2_SCALE = DH**-0.5 * math.log2(math.e)
MASKED = -1e30
VMEM_BYTES = 60 * 1024 * 1024
MESH = pl.DeviceIdType.MESH
F32 = jnp.float32
BF16 = jnp.bfloat16


def ctx_orders(bits, heads):
    far = list(range(bits - 1, 0, -1))
    return [(far if head % 2 == 0 else far[::-1]) + [0] for head in range(heads)]


def body(sizes, pick_ref, q_hbm, k_hbm, v_hbm, column_ref, row_ref, o_hbm, *scratch):
    tok, heads, bands, tp, count, group = sizes
    (kv, qs, outs, vert_sum, vk, vv, marks, joined, win, mark_win) = scratch[:10]
    (kv_loc, kv_snd, kv_rcv, q_loc, q_snd, q_rcv, c_snd, c_rcv, o_sem) = scratch[10:]
    part = tok // tp
    step = group * DH
    bits = max((count - 1).bit_length(), 1)
    me_c = lax.axis_index("ctx")
    me_t = lax.axis_index("tp")

    def across(bit):
        weight = 1 << bit
        return me_c + weight - 2 * weight * ((me_c // weight) % 2)

    ring = [lax.rem(me_t + k, tp) for k in range(tp)]
    peers = [(me_c, ring[k]) for k in range(1, tp)] + [(across(b), me_t) for b in range(bits)]
    barrier = pltpu.get_barrier_semaphore()
    for peer in peers:
        pl.semaphore_signal(barrier, inc=1, device_id=peer, device_id_type=MESH)
    pl.semaphore_wait(barrier, len(peers))

    own_rows = pl.ds(pl.multiple_of(me_t * part, part), part)

    def kv_copy(k, head, side):
        source = (k_hbm, v_hbm)[side]
        first = pl.multiple_of((ring[k] * heads + head) * DH, DH)
        source = source.at[:, pl.ds(first, DH)]
        target = kv.at[head, own_rows, pl.ds(side * DH, DH)]
        if k == 0:
            return pltpu.make_async_copy(source, target, kv_loc.at[head, side])
        return pltpu.make_async_remote_copy(
            src_ref=source,
            dst_ref=target,
            send_sem=kv_snd.at[k - 1, head, side],
            recv_sem=kv_rcv.at[k - 1, head, side],
            device_id=(me_c, ring[k]),
            device_id_type=MESH,
        )

    def q_copy(k, chunk):
        first = pl.multiple_of(ring[k] * (CHUNKS * step) + chunk * step, step)
        source = q_hbm.at[:, pl.ds(first, step)]
        target = qs.at[chunk, own_rows]
        if k == 0:
            return pltpu.make_async_copy(source, target, q_loc.at[chunk])
        return pltpu.make_async_remote_copy(
            src_ref=source,
            dst_ref=target,
            send_sem=q_snd.at[k - 1, chunk],
            recv_sem=q_rcv.at[k - 1, chunk],
            device_id=(me_c, ring[k]),
            device_id_type=MESH,
        )

    def ctx_copy(head, slot, bit):
        there = slot ^ (1 << bit)
        return pltpu.make_async_remote_copy(
            src_ref=kv.at[head, pl.ds(slot * tok, tok)],
            dst_ref=kv.at[head, pl.ds(there * tok, tok)],
            send_sem=c_snd.at[head, there],
            recv_sem=c_rcv.at[head, there],
            device_id=(across(bit), me_t),
            device_id_type=MESH,
        )

    sent = []

    def start_q(chunk):
        for k in range(tp - 1, 0, -1):
            copy = q_copy(k, chunk)
            copy.start()
            sent.append(copy)

    def add_vertical(head, slot):
        def one_block(index, carry):
            block = slot * (tok // PB) + index
            base = block * PB
            rows = kv[head, pl.ds(pl.multiple_of(base, PB), PB), :]
            lanes = lax.broadcasted_iota(jnp.int32, (VT, PB), 1) + base
            seen = jnp.zeros((1, PB), F32)
            for tile in range(vk.shape[1] // VT):
                span = pl.ds(tile * VT, VT)
                hit = jnp.where(column_ref[head, span, :] == lanes, 1.0, 0.0)
                seen += jnp.sum(hit, axis=0, keepdims=True)
                vert_sum[head, span, :] += jnp.dot(
                    hit.astype(BF16), rows, preferred_element_type=F32
                )
            for piece in range(PB // SUB):
                marks[head, pl.ds(block * (PB // SUB) + piece, 1), :] = seen[
                    :, piece * SUB : (piece + 1) * SUB
                ]
            return carry

        lax.fori_loop(0, tok // PB, one_block, 0)

    for head in range(heads):
        for side in range(2):
            for k in range(tp - 1, 0, -1):
                copy = kv_copy(k, head, side)
                copy.start()
                sent.append(copy)
            kv_copy(0, head, side).start()
    for chunk in range(CHUNKS):
        q_copy(0, chunk).start()
    vert_sum[...] = jnp.zeros_like(vert_sum)

    orders = ctx_orders(bits, heads)
    for head in range(heads):
        for side in range(2):
            kv_copy(0, head, side).wait()
            for k in range(1, tp):
                kv_copy(k, head, side).wait_recv()
        for bit in orders[head]:
            copy = ctx_copy(head, 0, bit)
            copy.start()
            sent.append(copy)
    start_q(0)
    for head in range(heads):
        add_vertical(head, 0)
    held = [[0] for _ in range(heads)]
    for turn in range(bits):
        fresh = [[slot ^ (1 << orders[head][turn]) for slot in held[head]] for head in range(heads)]
        for index in range(len(fresh[0])):
            for head in range(heads):
                ctx_copy(head, held[head][index], orders[head][turn]).wait_recv()
                for bit in orders[head][turn + 1 :]:
                    copy = ctx_copy(head, fresh[head][index], bit)
                    copy.start()
                    sent.append(copy)
        if turn < 2:
            start_q(1 + turn)
        for head in range(heads):
            for slot in fresh[head]:
                add_vertical(head, slot)
            held[head] += fresh[head]
    for chunk in range(1 + min(bits, 2), CHUNKS):
        start_q(chunk)

    for head in range(heads):
        vk[head] = vert_sum[head, :, :DH].astype(BF16)
        vv[head, :, :DH] = vert_sum[head, :, DH:].astype(BF16)
        vv[head, :, DH:] = jnp.ones((vv.shape[1], DH), BF16)

    per_dev = tok // SUB
    shifts = [1 << b for b in reversed(range(per_dev.bit_length() - 1))]

    def cut_window(head, band):
        entry = (head * bands + band) * (2 + len(shifts))
        picks = [pick_ref[entry + i] for i in range(2 + len(shifts))]

        def join(index, carry):
            piece = pl.multiple_of(index * SUB, SUB)
            both = [jnp.zeros((SUB, 2 * DH), BF16)] * 2
            for slot in range(count):
                rows = kv[head, pl.ds(slot * tok + piece, SUB), :]
                both = [lax.select(picks[i] == slot, rows, both[i]) for i in range(2)]
            for i in range(2):
                joined[pl.ds(i * tok + piece, SUB), :] = both[i]
            return carry

        lax.fori_loop(0, per_dev, join, 0)
        for turn, shift in enumerate(shifts):
            last = turn == len(shifts) - 1

            def move(index, carry):
                here = pl.ds(pl.multiple_of(index * SUB, SUB), SUB)
                there = pl.ds(pl.multiple_of((index + shift) * SUB, SUB), SUB)
                rows = lax.select(picks[2 + turn] == 1, joined[there, :], joined[here, :])
                if last:
                    win[head, band, here, :] = rows
                else:
                    joined[here, :] = rows
                return carry

            lax.fori_loop(0, per_dev + shift, move, 0)
        both = [jnp.ones((per_dev, SUB), F32)] * 2
        for slot in range(count):
            rows = marks[head, slot * per_dev : (slot + 1) * per_dev, :]
            both = [lax.select(picks[i] == slot, rows, both[i]) for i in range(2)]
        both = jnp.concatenate(both, axis=0)
        for turn, shift in enumerate(shifts):
            moved = jnp.concatenate((both[shift:], both[:shift]), axis=0)
            both = lax.select(picks[2 + turn] == 1, moved, both)
        mark_win[head, band] = both

    for head in range(heads):
        for band in range(bands):
            cut_window(head, band)

    rows = group * SUB
    slots = 4 * SUB
    nt = (((1,), (1,)), ((), ()))

    def attend(chunk, head, sub):
        upper = (
            lax.broadcasted_iota(jnp.int32, (rows, slots), 1) % SUB
            > lax.broadcasted_iota(jnp.int32, (rows, slots), 0) % SUB
        )
        ones = jnp.ones((slots, DH), BF16)
        sides = []
        for back in (1, 0):
            blocks, biases = [], []
            for band in range(bands):
                first = pl.multiple_of((sub + 1 - back) * SUB, SUB)
                blocks.append(win[head, band, pl.ds(first, SUB), :])
                if band == 0 and back == 0:
                    biases.append(jnp.zeros((1, SUB), F32))
                else:
                    gone = mark_win[head, band, pl.ds(sub + 1 - back, 1), :]
                    biases.append(jnp.where(gone > 0.5, MASKED, 0.0))
            for _ in range(4 - bands):
                blocks.append(jnp.zeros((SUB, 2 * DH), BF16))
                biases.append(jnp.full((1, SUB), MASKED, F32))
            sides.append((jnp.concatenate(blocks, axis=0), jnp.concatenate(biases, axis=1)))
        (near, near_bias), (own, own_bias) = sides
        here = pl.ds(pl.multiple_of(sub * SUB, SUB), SUB)
        q = jnp.concatenate(
            [qs[chunk, here, g * DH : (g + 1) * DH] for g in range(group)], axis=0
        )
        vert_bias = jnp.where(row_ref[head] < me_c * tok + sub * SUB, 0.0, MASKED)
        vert = lax.dot_general(q, vk[head], nt, preferred_element_type=F32) + vert_bias
        s_near = lax.dot_general(q, near[:, :DH], nt, preferred_element_type=F32)
        s_own = lax.dot_general(q, own[:, :DH], nt, preferred_element_type=F32)
        band = jnp.where(upper, s_near + near_bias, s_own + own_bias)
        top = jnp.maximum(
            jnp.max(vert, axis=1, keepdims=True), jnp.max(band, axis=1, keepdims=True)
        )
        p_vert = jnp.exp2((vert - top) * EXP2_SCALE).astype(BF16)
        p_band = jnp.exp2((band - top) * EXP2_SCALE)
        p_near = jnp.where(upper, p_band, 0.0).astype(BF16)
        p_own = jnp.where(upper, 0.0, p_band).astype(BF16)
        near_v = jnp.concatenate((near[:, DH:], ones), axis=1)
        own_v = jnp.concatenate((own[:, DH:], ones), axis=1)
        acc = jnp.dot(p_vert, vv[head], preferred_element_type=F32)
        acc += jnp.dot(p_near, near_v, preferred_element_type=F32)
        acc += jnp.dot(p_own, own_v, preferred_element_type=F32)
        out = (acc[:, :DH] / acc[:, DH:]).astype(BF16)
        for g in range(group):
            outs[chunk, here, g * DH : (g + 1) * DH] = out[g * SUB : (g + 1) * SUB]

    def out_copy(chunk):
        return pltpu.make_async_copy(
            outs.at[chunk], o_hbm.at[:, pl.ds(chunk * step, step)], o_sem.at[chunk]
        )

    for chunk in range(CHUNKS):
        q_copy(0, chunk).wait()
        for k in range(1, tp):
            q_copy(k, chunk).wait_recv()
        head = chunk * heads // CHUNKS

        def pair(index, carry):
            attend(chunk, head, index * 2)
            attend(chunk, head, index * 2 + 1)
            return carry

        lax.fori_loop(0, tok // SUB // 2, pair, 0)
        out_copy(chunk).start()
    for chunk in range(CHUNKS):
        out_copy(chunk).wait()
    for copy in sent:
        copy.wait_send()


def shards(queries, key_rows, value_rows, vertical_keys, slash_offsets):
    heads, vert_count = vertical_keys.shape
    bands = slash_offsets.shape[1]
    part = queries.shape[0]
    tp = lax.axis_size("tp")
    count = lax.axis_size("ctx")
    tok = part * tp
    total = tok * count
    me = lax.axis_index("ctx").astype(jnp.int32)
    width = queries.shape[1] // tp
    step = width // CHUNKS

    per_dev = tok // SUB
    start = me * per_dev - slash_offsets // SUB - 1
    low = start // per_dev
    rest = start % per_dev
    picks = [jnp.where(low + i >= 0, (low + i) ^ me, -1) for i in range(2)]
    picks += [(rest >> b) & 1 for b in reversed(range(per_dev.bit_length() - 1))]
    picks = jnp.stack(picks, axis=2).reshape(-1)
    column = (((vertical_keys // tok) ^ me) * tok + vertical_keys % tok)[:, :, None]

    vmem = pl.BlockSpec(memory_space=pltpu.VMEM)
    smem = pl.BlockSpec(memory_space=pltpu.SMEM)
    hbm = pl.BlockSpec(memory_space=pl.ANY)
    dma = pltpu.SemaphoreType.DMA
    scores = tok * (width // DH) * 1536
    return pl.pallas_call(
        functools.partial(body, (tok, heads, bands, tp, count, step // DH)),
        out_shape=jax.ShapeDtypeStruct((tok, width), BF16),
        in_specs=[smem, hbm, hbm, hbm, vmem, vmem],
        out_specs=hbm,
        scratch_shapes=[
            pltpu.VMEM((heads, total, 2 * DH), BF16),
            pltpu.VMEM((CHUNKS, tok, step), BF16),
            pltpu.VMEM((CHUNKS, tok, step), BF16),
            pltpu.VMEM((heads, vert_count, 2 * DH), F32),
            pltpu.VMEM((heads, vert_count, DH), BF16),
            pltpu.VMEM((heads, vert_count, 2 * DH), BF16),
            pltpu.VMEM((heads, total // SUB, SUB), F32),
            pltpu.VMEM((2 * tok, 2 * DH), BF16),
            pltpu.VMEM((heads, bands, tok + SUB, 2 * DH), BF16),
            pltpu.VMEM((heads, bands, 2 * tok // SUB, SUB), F32),
            dma((heads, 2)),
            dma((tp - 1, heads, 2)),
            dma((tp - 1, heads, 2)),
            dma((CHUNKS,)),
            dma((tp - 1, CHUNKS)),
            dma((tp - 1, CHUNKS)),
            dma((heads, count)),
            dma((heads, count)),
            dma((CHUNKS,)),
        ],
        compiler_params=pltpu.CompilerParams(
            collective_id=0, has_side_effects=True, vmem_limit_bytes=VMEM_BYTES
        ),
        cost_estimate=pl.CostEstimate(
            flops=scores * 1024, bytes_accessed=32 << 20, transcendentals=scores
        ),
        name="attend_all",
    )(picks, queries, key_rows, value_rows, column, vertical_keys[:, None, :])


def solution(mesh):
    in_specs = (
        P(("ctx", "tp"), None),
        P(("ctx", "tp"), None),
        P(("ctx", "tp"), None),
        P("tp", None),
        P("tp", None),
    )
    out_specs = P("ctx", "tp")
    return jax.shard_map(shards, mesh=mesh, in_specs=in_specs, out_specs=out_specs, check_vma=False)
```

```python
import functools
import math

import jax
import jax.numpy as jnp
from jax import lax
from jax.experimental import pallas as pl
from jax.experimental.pallas import tpu as pltpu
from jax.sharding import PartitionSpec as P

HQ = 64
KVH = 8
DH = 128
SUB = 64
HALVES = 2
VT = 256
PB = 512
EXP2_SCALE = DH**-0.5 * math.log2(math.e)
MASKED = -1e30
VMEM_BYTES = 60 * 1024 * 1024
MESH = pl.DeviceIdType.MESH
F32 = jnp.float32
BF16 = jnp.bfloat16


def ctx_orders(bits, heads):
    far = list(range(bits - 1, 0, -1))
    return [(far if head % 2 == 0 else far[::-1]) + [0] for head in range(heads)]


def body(sizes, pick_ref, q_hbm, k_hbm, v_hbm, column_ref, row_ref, o_hbm, *scratch):
    tok, heads, bands, tp, count, group = sizes
    (kv, qs, outs, vert_sum, vk, vv, marks, joined, win, mark_win) = scratch[:10]
    (kv_loc, kv_snd, kv_rcv, q_loc, q_snd, q_rcv, c_snd, c_rcv, o_sem) = scratch[10:]
    part = tok // tp
    step = group * DH
    share = part // HALVES
    chunks = heads * HALVES
    bits = max((count - 1).bit_length(), 1)
    me_c = lax.axis_index("ctx")
    me_t = lax.axis_index("tp")

    def across(bit):
        weight = 1 << bit
        return me_c + weight - 2 * weight * ((me_c // weight) % 2)

    ring = [lax.rem(me_t + k, tp) for k in range(tp)]
    peers = [(me_c, ring[k]) for k in range(1, tp)] + [(across(b), me_t) for b in range(bits)]
    barrier = pltpu.get_barrier_semaphore()
    for peer in peers:
        pl.semaphore_signal(barrier, inc=1, device_id=peer, device_id_type=MESH)
    pl.semaphore_wait(barrier, len(peers))

    own_rows = pl.ds(pl.multiple_of(me_t * part, part), part)

    def kv_copy(k, head, side):
        source = (k_hbm, v_hbm)[side]
        first = pl.multiple_of((ring[k] * heads + head) * DH, DH)
        source = source.at[:, pl.ds(first, DH)]
        target = kv.at[head, own_rows, pl.ds(side * DH, DH)]
        if k == 0:
            return pltpu.make_async_copy(source, target, kv_loc.at[head, side])
        return pltpu.make_async_remote_copy(
            src_ref=source,
            dst_ref=target,
            send_sem=kv_snd.at[k - 1, head, side],
            recv_sem=kv_rcv.at[k - 1, head, side],
            device_id=(me_c, ring[k]),
            device_id_type=MESH,
        )

    def q_copy(k, chunk):
        head, half = chunk // HALVES, chunk % HALVES
        first = pl.multiple_of((ring[k] * heads + head) * step, step)
        source = q_hbm.at[pl.ds(half * share, share), pl.ds(first, step)]
        landing = pl.multiple_of(me_t * part + half * share, share)
        target = qs.at[head, pl.ds(landing, share)]
        if k == 0:
            return pltpu.make_async_copy(source, target, q_loc.at[chunk])
        return pltpu.make_async_remote_copy(
            src_ref=source,
            dst_ref=target,
            send_sem=q_snd.at[k - 1, chunk],
            recv_sem=q_rcv.at[k - 1, chunk],
            device_id=(me_c, ring[k]),
            device_id_type=MESH,
        )

    def ctx_copy(head, slot, bit, k):
        there = slot ^ (1 << bit)
        quarter = lax.rem(me_t - k + tp, tp) * part
        return pltpu.make_async_remote_copy(
            src_ref=kv.at[head, pl.ds(pl.multiple_of(slot * tok + quarter, part), part)],
            dst_ref=kv.at[head, pl.ds(pl.multiple_of(there * tok + quarter, part), part)],
            send_sem=c_snd.at[head, there, k],
            recv_sem=c_rcv.at[head, there, k],
            device_id=(across(bit), me_t),
            device_id_type=MESH,
        )

    sent = []

    def start_q(chunk):
        for k in range(tp - 1, 0, -1):
            copy = q_copy(k, chunk)
            copy.start()
            sent.append(copy)

    def add_vertical(head, slot):
        def one_block(index, carry):
            block = slot * (tok // PB) + index
            base = block * PB
            rows = kv[head, pl.ds(pl.multiple_of(base, PB), PB), :]
            lanes = lax.broadcasted_iota(jnp.int32, (VT, PB), 1) + base
            seen = jnp.zeros((1, PB), F32)
            for tile in range(vk.shape[1] // VT):
                span = pl.ds(tile * VT, VT)
                hit = jnp.where(column_ref[head, span, :] == lanes, 1.0, 0.0)
                seen += jnp.sum(hit, axis=0, keepdims=True)
                vert_sum[head, span, :] += jnp.dot(
                    hit.astype(BF16), rows, preferred_element_type=F32
                )
            for piece in range(PB // SUB):
                marks[head, pl.ds(block * (PB // SUB) + piece, 1), :] = seen[
                    :, piece * SUB : (piece + 1) * SUB
                ]
            return carry

        lax.fori_loop(0, tok // PB, one_block, 0)

    for k in range(tp):
        for head in range(heads):
            for side in range(2):
                copy = kv_copy(k, head, side)
                copy.start()
                if k > 0:
                    sent.append(copy)
    for chunk in range(chunks):
        q_copy(0, chunk).start()
    vert_sum[...] = jnp.zeros_like(vert_sum)

    orders = ctx_orders(bits, heads)
    for k in range(tp):
        for head in range(heads):
            for side in range(2):
                if k == 0:
                    kv_copy(k, head, side).wait()
                else:
                    kv_copy(k, head, side).wait_recv()
            for bit in orders[head]:
                copy = ctx_copy(head, 0, bit, k)
                copy.start()
                sent.append(copy)
    start_q(0)
    for head in range(heads):
        add_vertical(head, 0)
    held = [[0] for _ in range(heads)]
    for turn in range(bits):
        fresh = [[slot ^ (1 << orders[head][turn]) for slot in held[head]] for head in range(heads)]
        for index in range(len(fresh[0])):
            for k in range(tp):
                for head in range(heads):
                    ctx_copy(head, held[head][index], orders[head][turn], k).wait_recv()
                    for bit in orders[head][turn + 1 :]:
                        copy = ctx_copy(head, fresh[head][index], bit, k)
                        copy.start()
                        sent.append(copy)
        if turn < 2:
            start_q(1 + turn)
        for head in range(heads):
            for slot in fresh[head]:
                add_vertical(head, slot)
            held[head] += fresh[head]
    for chunk in range(1 + min(bits, 2), chunks):
        start_q(chunk)

    for head in range(heads):
        vk[head] = vert_sum[head, :, :DH].astype(BF16)
        vv[head, :, :DH] = vert_sum[head, :, DH:].astype(BF16)
        vv[head, :, DH:] = jnp.ones((vv.shape[1], DH), BF16)

    per_dev = tok // SUB
    shifts = [1 << b for b in reversed(range(per_dev.bit_length() - 1))]

    def cut_window(head, band):
        entry = (head * bands + band) * (2 + len(shifts))
        picks = [pick_ref[entry + i] for i in range(2 + len(shifts))]

        def join(index, carry):
            piece = pl.multiple_of(index * SUB, SUB)
            both = [jnp.zeros((SUB, 2 * DH), BF16)] * 2
            for slot in range(count):
                rows = kv[head, pl.ds(slot * tok + piece, SUB), :]
                both = [lax.select(picks[i] == slot, rows, both[i]) for i in range(2)]
            for i in range(2):
                joined[pl.ds(i * tok + piece, SUB), :] = both[i]
            return carry

        lax.fori_loop(0, per_dev, join, 0)
        for turn, shift in enumerate(shifts):
            last = turn == len(shifts) - 1

            def move(index, carry):
                here = pl.ds(pl.multiple_of(index * SUB, SUB), SUB)
                there = pl.ds(pl.multiple_of((index + shift) * SUB, SUB), SUB)
                rows = lax.select(picks[2 + turn] == 1, joined[there, :], joined[here, :])
                if last:
                    win[head, band, here, :] = rows
                else:
                    joined[here, :] = rows
                return carry

            lax.fori_loop(0, per_dev + shift, move, 0)
        both = [jnp.ones((per_dev, SUB), F32)] * 2
        for slot in range(count):
            rows = marks[head, slot * per_dev : (slot + 1) * per_dev, :]
            both = [lax.select(picks[i] == slot, rows, both[i]) for i in range(2)]
        both = jnp.concatenate(both, axis=0)
        for turn, shift in enumerate(shifts):
            moved = jnp.concatenate((both[shift:], both[:shift]), axis=0)
            both = lax.select(picks[2 + turn] == 1, moved, both)
        mark_win[head, band] = both

    for head in range(heads):
        for band in range(bands):
            cut_window(head, band)

    rows = group * SUB
    slots = 4 * SUB
    nt = (((1,), (1,)), ((), ()))

    def scores(head, sub):
        upper = (
            lax.broadcasted_iota(jnp.int32, (rows, slots), 1) % SUB
            > lax.broadcasted_iota(jnp.int32, (rows, slots), 0) % SUB
        )
        ones = jnp.ones((slots, DH), BF16)
        sides = []
        for back in (1, 0):
            blocks, biases = [], []
            for band in range(bands):
                first = pl.multiple_of((sub + 1 - back) * SUB, SUB)
                blocks.append(win[head, band, pl.ds(first, SUB), :])
                if band == 0 and back == 0:
                    biases.append(jnp.zeros((1, SUB), F32))
                else:
                    gone = mark_win[head, band, pl.ds(sub + 1 - back, 1), :]
                    biases.append(jnp.where(gone > 0.5, MASKED, 0.0))
            for _ in range(4 - bands):
                blocks.append(jnp.zeros((SUB, 2 * DH), BF16))
                biases.append(jnp.full((1, SUB), MASKED, F32))
            sides.append((jnp.concatenate(blocks, axis=0), jnp.concatenate(biases, axis=1)))
        (near, near_bias), (own, own_bias) = sides
        here = pl.ds(pl.multiple_of(sub * SUB, SUB), SUB)
        q = jnp.concatenate(
            [qs[head, here, g * DH : (g + 1) * DH] for g in range(group)], axis=0
        )
        vert_bias = jnp.where(row_ref[head : head + 1, :] < me_c * tok + sub * SUB, 0.0, MASKED)
        vert = lax.dot_general(q, vk[head], nt, preferred_element_type=F32) + vert_bias
        s_near = lax.dot_general(q, near[:, :DH], nt, preferred_element_type=F32)
        s_own = lax.dot_general(q, own[:, :DH], nt, preferred_element_type=F32)
        band = jnp.where(upper, s_near + near_bias, s_own + own_bias)
        near_v = jnp.concatenate((near[:, DH:], ones), axis=1)
        own_v = jnp.concatenate((own[:, DH:], ones), axis=1)
        return vert, band, upper, near_v, own_v

    def finish(head, sub, vert, band, upper, near_v, own_v):
        top = jnp.maximum(
            jnp.max(vert, axis=1, keepdims=True), jnp.max(band, axis=1, keepdims=True)
        )
        p_vert = jnp.exp2((vert - top) * EXP2_SCALE).astype(BF16)
        p_band = jnp.exp2((band - top) * EXP2_SCALE)
        p_near = jnp.where(upper, p_band, 0.0).astype(BF16)
        p_own = jnp.where(upper, 0.0, p_band).astype(BF16)
        acc = jnp.dot(p_vert, vv[head], preferred_element_type=F32)
        acc += jnp.dot(p_near, near_v, preferred_element_type=F32)
        acc += jnp.dot(p_own, own_v, preferred_element_type=F32)
        out = (acc[:, :DH] / acc[:, DH:]).astype(BF16)
        here = pl.ds(pl.multiple_of(sub * SUB, SUB), SUB)
        for g in range(group):
            outs[head, here, g * DH : (g + 1) * DH] = out[g * SUB : (g + 1) * SUB]

    def out_copy(head, half, source):
        here = pl.ds(pl.multiple_of(source * part + half * share, share), share)
        return pltpu.make_async_copy(
            outs.at[head, here],
            o_hbm.at[here, pl.ds(head * step, step)],
            o_sem.at[head * HALVES + half, source],
        )

    for chunk in range(chunks):
        q_copy(0, chunk).wait()
        for k in range(1, tp):
            q_copy(k, chunk).wait_recv()
        head, half = chunk // HALVES, chunk % HALVES

        def one_source(source, carry):
            first = (source * part + half * share) // SUB
            subs = [first + i for i in range(share // SUB)]
            ready = [scores(head, sub) for sub in subs]
            for sub, parts in zip(subs, ready):
                finish(head, sub, *parts)
            out_copy(head, half, source).start()
            return carry

        lax.fori_loop(0, tp, one_source, 0)
    for chunk in range(chunks):
        for source in range(tp):
            out_copy(chunk // HALVES, chunk % HALVES, source).wait()
    for copy in sent:
        copy.wait_send()


def shards(queries, key_rows, value_rows, vertical_keys, slash_offsets):
    heads, vert_count = vertical_keys.shape
    bands = slash_offsets.shape[1]
    part = queries.shape[0]
    tp = lax.axis_size("tp")
    count = lax.axis_size("ctx")
    tok = part * tp
    total = tok * count
    me = lax.axis_index("ctx").astype(jnp.int32)
    width = queries.shape[1] // tp
    step = width // heads
    chunks = heads * HALVES

    per_dev = tok // SUB
    start = me * per_dev - slash_offsets // SUB - 1
    low = start // per_dev
    rest = start % per_dev
    picks = [jnp.where(low + i >= 0, (low + i) ^ me, -1) for i in range(2)]
    picks += [(rest >> b) & 1 for b in reversed(range(per_dev.bit_length() - 1))]
    picks = jnp.stack(picks, axis=2).reshape(-1)
    column = (((vertical_keys // tok) ^ me) * tok + vertical_keys % tok)[:, :, None]

    vmem = pl.BlockSpec(memory_space=pltpu.VMEM)
    smem = pl.BlockSpec(memory_space=pltpu.SMEM)
    hbm = pl.BlockSpec(memory_space=pl.ANY)
    dma = pltpu.SemaphoreType.DMA
    scores = tok * (width // DH) * 1536
    return pl.pallas_call(
        functools.partial(body, (tok, heads, bands, tp, count, step // DH)),
        out_shape=jax.ShapeDtypeStruct((tok, width), BF16),
        in_specs=[smem, hbm, hbm, hbm, vmem, vmem],
        out_specs=hbm,
        scratch_shapes=[
            pltpu.VMEM((heads, total, 2 * DH), BF16),
            pltpu.VMEM((heads, tok, step), BF16),
            pltpu.VMEM((heads, tok, step), BF16),
            pltpu.VMEM((heads, vert_count, 2 * DH), F32),
            pltpu.VMEM((heads, vert_count, DH), BF16),
            pltpu.VMEM((heads, vert_count, 2 * DH), BF16),
            pltpu.VMEM((heads, total // SUB, SUB), F32),
            pltpu.VMEM((2 * tok, 2 * DH), BF16),
            pltpu.VMEM((heads, bands, tok + SUB, 2 * DH), BF16),
            pltpu.VMEM((heads, bands, 2 * tok // SUB, SUB), F32),
            dma((heads, 2)),
            dma((tp - 1, heads, 2)),
            dma((tp - 1, heads, 2)),
            dma((chunks,)),
            dma((tp - 1, chunks)),
            dma((tp - 1, chunks)),
            dma((heads, count, tp)),
            dma((heads, count, tp)),
            dma((chunks, tp)),
        ],
        compiler_params=pltpu.CompilerParams(
            collective_id=0, has_side_effects=True, vmem_limit_bytes=VMEM_BYTES
        ),
        cost_estimate=pl.CostEstimate(
            flops=scores * 1024, bytes_accessed=32 << 20, transcendentals=scores
        ),
        name="attend_all",
    )(picks, queries, key_rows, value_rows, column, vertical_keys)


def solution(mesh):
    in_specs = (
        P(("ctx", "tp"), None),
        P(("ctx", "tp"), None),
        P(("ctx", "tp"), None),
        P("tp", None),
        P("tp", None),
    )
    out_specs = P("ctx", "tp")
    return jax.shard_map(shards, mesh=mesh, in_specs=in_specs, out_specs=out_specs, check_vma=False)
```

```python
import functools
import math

import jax
import jax.numpy as jnp
from jax import lax
from jax.experimental import pallas as pl
from jax.experimental.pallas import tpu as pltpu
from jax.sharding import PartitionSpec as P

HQ = 64
KVH = 8
DH = 128
SUB = 64
HALVES = 2
VT = 256
PB = 512
EXP2_SCALE = DH**-0.5 * math.log2(math.e)
MASKED = -1e30
VMEM_BYTES = 60 * 1024 * 1024
MESH = pl.DeviceIdType.MESH
F32 = jnp.float32
BF16 = jnp.bfloat16


def ctx_orders(bits, heads):
    far = list(range(bits - 1, 0, -1))
    return [(far if head % 2 == 0 else far[::-1]) + [0] for head in range(heads)]


def body(sizes, pick_ref, q_hbm, k_hbm, v_hbm, column_ref, row_ref, o_hbm, *scratch):
    tok, heads, bands, tp, count, group = sizes
    (kv, qs, outs, vert_sum, vk, vv, marks, joined, win, mark_win) = scratch[:10]
    (kv_loc, kv_snd, kv_rcv, q_loc, q_snd, q_rcv, c_snd, c_rcv, o_sem) = scratch[10:]
    part = tok // tp
    step = group * DH
    share = part // HALVES
    chunks = heads * HALVES
    bits = max((count - 1).bit_length(), 1)
    me_c = lax.axis_index("ctx")
    me_t = lax.axis_index("tp")

    def across(bit):
        weight = 1 << bit
        return me_c + weight - 2 * weight * ((me_c // weight) % 2)

    ring = [lax.rem(me_t + k, tp) for k in range(tp)]
    peers = [(me_c, ring[k]) for k in range(1, tp)] + [(across(b), me_t) for b in range(bits)]
    barrier = pltpu.get_barrier_semaphore()
    for peer in peers:
        pl.semaphore_signal(barrier, inc=1, device_id=peer, device_id_type=MESH)
    pl.semaphore_wait(barrier, len(peers))

    own_rows = pl.ds(pl.multiple_of(me_t * part, part), part)

    def kv_copy(k, head, side):
        source = (k_hbm, v_hbm)[side]
        first = pl.multiple_of((ring[k] * heads + head) * DH, DH)
        source = source.at[:, pl.ds(first, DH)]
        target = kv.at[head, own_rows, pl.ds(side * DH, DH)]
        if k == 0:
            return pltpu.make_async_copy(source, target, kv_loc.at[head, side])
        return pltpu.make_async_remote_copy(
            src_ref=source,
            dst_ref=target,
            send_sem=kv_snd.at[k - 1, head, side],
            recv_sem=kv_rcv.at[k - 1, head, side],
            device_id=(me_c, ring[k]),
            device_id_type=MESH,
        )

    def q_copy(k, chunk):
        head, half = chunk // HALVES, chunk % HALVES
        other = lax.rem(me_t + k, tp)
        first = pl.multiple_of((other * heads + head) * step, step)
        source = q_hbm.at[pl.ds(half * share, share), pl.ds(first, step)]
        landing = pl.multiple_of(me_t * part + half * share, share)
        target = qs.at[head, pl.ds(landing, share)]
        if isinstance(k, int) and k == 0:
            return pltpu.make_async_copy(source, target, q_loc.at[chunk])
        return pltpu.make_async_remote_copy(
            src_ref=source,
            dst_ref=target,
            send_sem=q_snd.at[k - 1, chunk],
            recv_sem=q_rcv.at[k - 1, chunk],
            device_id=(me_c, other),
            device_id_type=MESH,
        )

    def ctx_copy(head, slot, bit, k):
        there = slot ^ (1 << bit)
        quarter = lax.rem(me_t - k + tp, tp) * part
        return pltpu.make_async_remote_copy(
            src_ref=kv.at[head, pl.ds(pl.multiple_of(slot * tok + quarter, part), part)],
            dst_ref=kv.at[head, pl.ds(pl.multiple_of(there * tok + quarter, part), part)],
            send_sem=c_snd.at[head, there, k],
            recv_sem=c_rcv.at[head, there, k],
            device_id=(across(bit), me_t),
            device_id_type=MESH,
        )

    sent = []

    def start_q(chunk):
        for k in range(1, tp):
            copy = q_copy(k, chunk)
            copy.start()
            sent.append(copy)

    def add_vertical(head, slot):
        def one_block(index, carry):
            block = slot * (tok // PB) + index
            base = block * PB
            rows = kv[head, pl.ds(pl.multiple_of(base, PB), PB), :]
            lanes = lax.broadcasted_iota(jnp.int32, (VT, PB), 1) + base
            seen = jnp.zeros((1, PB), F32)
            for tile in range(vk.shape[1] // VT):
                span = pl.ds(tile * VT, VT)
                hit = jnp.where(column_ref[head, span, :] == lanes, 1.0, 0.0)
                seen += jnp.sum(hit, axis=0, keepdims=True)
                vert_sum[head, span, :] += jnp.dot(
                    hit.astype(BF16), rows, preferred_element_type=F32
                )
            for piece in range(PB // SUB):
                marks[head, pl.ds(block * (PB // SUB) + piece, 1), :] = seen[
                    :, piece * SUB : (piece + 1) * SUB
                ]
            return carry

        lax.fori_loop(0, tok // PB, one_block, 0)

    for k in range(tp):
        for head in range(heads):
            for side in range(2):
                copy = kv_copy(k, head, side)
                copy.start()
                if k > 0:
                    sent.append(copy)
    for chunk in range(chunks):
        q_copy(0, chunk).start()
    vert_sum[...] = jnp.zeros_like(vert_sum)

    orders = ctx_orders(bits, heads)
    for k in range(tp):
        for head in range(heads):
            for side in range(2):
                if k == 0:
                    kv_copy(k, head, side).wait()
                else:
                    kv_copy(k, head, side).wait_recv()
            for bit in orders[head]:
                copy = ctx_copy(head, 0, bit, k)
                copy.start()
                sent.append(copy)
    for chunk in range(2):
        start_q(chunk)
    for head in range(heads):
        add_vertical(head, 0)
    held = [[0] for _ in range(heads)]
    for turn in range(bits):
        fresh = [[slot ^ (1 << orders[head][turn]) for slot in held[head]] for head in range(heads)]
        for index in range(len(fresh[0])):
            for k in range(tp):
                for head in range(heads):
                    ctx_copy(head, held[head][index], orders[head][turn], k).wait_recv()
                    for bit in orders[head][turn + 1 :]:
                        copy = ctx_copy(head, fresh[head][index], bit, k)
                        copy.start()
                        sent.append(copy)
        if 2 + turn < chunks:
            start_q(2 + turn)
        for head in range(heads):
            for slot in fresh[head]:
                add_vertical(head, slot)
            held[head] += fresh[head]
    for chunk in range(2 + bits, chunks):
        start_q(chunk)

    per_dev = tok // SUB
    shifts = [1 << b for b in reversed(range(per_dev.bit_length() - 1))]

    def cut_window(head, band):
        entry = (head * bands + band) * (2 + len(shifts))
        picks = [pick_ref[entry + i] for i in range(2 + len(shifts))]

        def join(index, carry):
            piece = pl.multiple_of(index * SUB, SUB)
            both = [jnp.zeros((SUB, 2 * DH), BF16)] * 2
            for slot in range(count):
                rows = kv[head, pl.ds(slot * tok + piece, SUB), :]
                both = [lax.select(picks[i] == slot, rows, both[i]) for i in range(2)]
            for i in range(2):
                joined[pl.ds(i * tok + piece, SUB), :] = both[i]
            return carry

        lax.fori_loop(0, per_dev, join, 0)
        for turn, shift in enumerate(shifts):
            last = turn == len(shifts) - 1

            def move(index, carry):
                here = pl.ds(pl.multiple_of(index * SUB, SUB), SUB)
                there = pl.ds(pl.multiple_of((index + shift) * SUB, SUB), SUB)
                rows = lax.select(picks[2 + turn] == 1, joined[there, :], joined[here, :])
                if last:
                    win[head, band, here, :] = rows
                else:
                    joined[here, :] = rows
                return carry

            lax.fori_loop(0, per_dev + shift, move, 0)
        both = [jnp.ones((per_dev, SUB), F32)] * 2
        for slot in range(count):
            rows = marks[head, slot * per_dev : (slot + 1) * per_dev, :]
            both = [lax.select(picks[i] == slot, rows, both[i]) for i in range(2)]
        both = jnp.concatenate(both, axis=0)
        for turn, shift in enumerate(shifts):
            moved = jnp.concatenate((both[shift:], both[:shift]), axis=0)
            both = lax.select(picks[2 + turn] == 1, moved, both)
        mark_win[head, band] = both

    def prepare(head):
        vk[head] = vert_sum[head, :, :DH].astype(BF16)
        vv[head, :, :DH] = vert_sum[head, :, DH:].astype(BF16)
        vv[head, :, DH:] = jnp.ones((vv.shape[1], DH), BF16)
        for band in range(bands):
            cut_window(head, band)

    rows = group * SUB
    slots = 4 * SUB
    nt = (((1,), (1,)), ((), ()))

    def scores(head, sub):
        upper = (
            lax.broadcasted_iota(jnp.int32, (rows, slots), 1) % SUB
            > lax.broadcasted_iota(jnp.int32, (rows, slots), 0) % SUB
        )
        ones = jnp.ones((slots, DH), BF16)
        sides = []
        for back in (1, 0):
            blocks, biases = [], []
            for band in range(bands):
                first = pl.multiple_of((sub + 1 - back) * SUB, SUB)
                blocks.append(win[head, band, pl.ds(first, SUB), :])
                if band == 0 and back == 0:
                    biases.append(jnp.zeros((1, SUB), F32))
                else:
                    gone = mark_win[head, band, pl.ds(sub + 1 - back, 1), :]
                    biases.append(jnp.where(gone > 0.5, MASKED, 0.0))
            for _ in range(4 - bands):
                blocks.append(jnp.zeros((SUB, 2 * DH), BF16))
                biases.append(jnp.full((1, SUB), MASKED, F32))
            sides.append((jnp.concatenate(blocks, axis=0), jnp.concatenate(biases, axis=1)))
        (near, near_bias), (own, own_bias) = sides
        here = pl.ds(pl.multiple_of(sub * SUB, SUB), SUB)
        q = jnp.concatenate(
            [qs[head, here, g * DH : (g + 1) * DH] for g in range(group)], axis=0
        )
        vert_bias = jnp.where(row_ref[head : head + 1, :] < me_c * tok + sub * SUB, 0.0, MASKED)
        vert = lax.dot_general(q, vk[head], nt, preferred_element_type=F32) + vert_bias
        s_near = lax.dot_general(q, near[:, :DH], nt, preferred_element_type=F32)
        s_own = lax.dot_general(q, own[:, :DH], nt, preferred_element_type=F32)
        band = jnp.where(upper, s_near + near_bias, s_own + own_bias)
        near_v = jnp.concatenate((near[:, DH:], ones), axis=1)
        own_v = jnp.concatenate((own[:, DH:], ones), axis=1)
        return vert, band, upper, near_v, own_v

    def finish(head, sub, vert, band, upper, near_v, own_v):
        top = jnp.maximum(
            jnp.max(vert, axis=1, keepdims=True), jnp.max(band, axis=1, keepdims=True)
        )
        p_vert = jnp.exp2((vert - top) * EXP2_SCALE).astype(BF16)
        p_band = jnp.exp2((band - top) * EXP2_SCALE)
        p_near = jnp.where(upper, p_band, 0.0).astype(BF16)
        p_own = jnp.where(upper, 0.0, p_band).astype(BF16)
        acc = jnp.dot(p_vert, vv[head], preferred_element_type=F32)
        acc += jnp.dot(p_near, near_v, preferred_element_type=F32)
        acc += jnp.dot(p_own, own_v, preferred_element_type=F32)
        out = (acc[:, :DH] / acc[:, DH:]).astype(BF16)
        here = pl.ds(pl.multiple_of(sub * SUB, SUB), SUB)
        for g in range(group):
            outs[head, here, g * DH : (g + 1) * DH] = out[g * SUB : (g + 1) * SUB]

    def out_copy(head, half, source):
        here = pl.ds(pl.multiple_of(source * part + half * share, share), share)
        return pltpu.make_async_copy(
            outs.at[head, here],
            o_hbm.at[here, pl.ds(head * step, step)],
            o_sem.at[head * HALVES + half, source],
        )

    def one_source(head, half, source):
        first = (source * part + half * share) // SUB
        subs = [first + i for i in range(share // SUB)]
        ready = [scores(head, sub) for sub in subs]
        for sub, parts in zip(subs, ready):
            finish(head, sub, *parts)
        out_copy(head, half, source).start()

    for chunk in range(chunks):
        head, half = chunk // HALVES, chunk % HALVES
        if half == 0:
            prepare(head)
        q_copy(0, chunk).wait()
        one_source(head, half, me_t)

        def arrived(k, carry):
            q_copy(k, chunk).wait_recv()
            one_source(head, half, lax.rem(me_t - k + tp, tp))
            return carry

        lax.fori_loop(1, tp, arrived, 0)
    for chunk in range(chunks):
        for source in range(tp):
            out_copy(chunk // HALVES, chunk % HALVES, source).wait()
    for copy in sent:
        copy.wait_send()


def shards(queries, key_rows, value_rows, vertical_keys, slash_offsets):
    heads, vert_count = vertical_keys.shape
    bands = slash_offsets.shape[1]
    part = queries.shape[0]
    tp = lax.axis_size("tp")
    count = lax.axis_size("ctx")
    tok = part * tp
    total = tok * count
    me = lax.axis_index("ctx").astype(jnp.int32)
    width = queries.shape[1] // tp
    step = width // heads
    chunks = heads * HALVES

    per_dev = tok // SUB
    start = me * per_dev - slash_offsets // SUB - 1
    low = start // per_dev
    rest = start % per_dev
    picks = [jnp.where(low + i >= 0, (low + i) ^ me, -1) for i in range(2)]
    picks += [(rest >> b) & 1 for b in reversed(range(per_dev.bit_length() - 1))]
    picks = jnp.stack(picks, axis=2).reshape(-1)
    column = (((vertical_keys // tok) ^ me) * tok + vertical_keys % tok)[:, :, None]

    vmem = pl.BlockSpec(memory_space=pltpu.VMEM)
    smem = pl.BlockSpec(memory_space=pltpu.SMEM)
    hbm = pl.BlockSpec(memory_space=pl.ANY)
    dma = pltpu.SemaphoreType.DMA
    scores = tok * (width // DH) * 1536
    return pl.pallas_call(
        functools.partial(body, (tok, heads, bands, tp, count, step // DH)),
        out_shape=jax.ShapeDtypeStruct((tok, width), BF16),
        in_specs=[smem, hbm, hbm, hbm, vmem, vmem],
        out_specs=hbm,
        scratch_shapes=[
            pltpu.VMEM((heads, total, 2 * DH), BF16),
            pltpu.VMEM((heads, tok, step), BF16),
            pltpu.VMEM((heads, tok, step), BF16),
            pltpu.VMEM((heads, vert_count, 2 * DH), F32),
            pltpu.VMEM((heads, vert_count, DH), BF16),
            pltpu.VMEM((heads, vert_count, 2 * DH), BF16),
            pltpu.VMEM((heads, total // SUB, SUB), F32),
            pltpu.VMEM((2 * tok, 2 * DH), BF16),
            pltpu.VMEM((heads, bands, tok + SUB, 2 * DH), BF16),
            pltpu.VMEM((heads, bands, 2 * tok // SUB, SUB), F32),
            dma((heads, 2)),
            dma((tp - 1, heads, 2)),
            dma((tp - 1, heads, 2)),
            dma((chunks,)),
            dma((tp - 1, chunks)),
            dma((tp - 1, chunks)),
            dma((heads, count, tp)),
            dma((heads, count, tp)),
            dma((chunks, tp)),
        ],
        compiler_params=pltpu.CompilerParams(
            collective_id=0, has_side_effects=True, vmem_limit_bytes=VMEM_BYTES
        ),
        cost_estimate=pl.CostEstimate(
            flops=scores * 1024, bytes_accessed=32 << 20, transcendentals=scores
        ),
        name="attend_all",
    )(picks, queries, key_rows, value_rows, column, vertical_keys)


def solution(mesh):
    in_specs = (
        P(("ctx", "tp"), None),
        P(("ctx", "tp"), None),
        P(("ctx", "tp"), None),
        P("tp", None),
        P("tp", None),
    )
    out_specs = P("ctx", "tp")
    return jax.shard_map(shards, mesh=mesh, in_specs=in_specs, out_specs=out_specs, check_vma=False)
```
